256 devices in a mesh: tile: 128 (over z, x, y_hi, core), group: 2 (over y_lo).
Axes of the slice: x: 4, y: 4 (y_hi: 2, y_lo: 2; y = y_hi * 2 + y_lo), z: 8, core: 2. Of those that a mesh axis runs over, the one named last changes fastest.
Arguments:
- state: float32 [8, 5, 128, 128, 128], P('group', None, 'tile'), may hold values from -6 to 6
- courant_x: float32 [8], P('group'), may hold values from -0.35 to 0.35
- courant_y: float32 [8], P('group'), may hold values from -0.35 to 0.35
- diffusion: float32 [5], replicated, may hold values from 0.02 to 0.07
- neighbours: int32 [9, 128, 128, 128], P(None, 'tile'), may hold values from 0 to 16899, as said below
- w_in: bfloat16 [360, 256], replicated, may hold values from -0.3125 to 0.3125
- w_mid: bfloat16 [256, 256], replicated, may hold values from -0.375 to 0.375
- w_out: bfloat16 [256, 40], replicated, may hold values from -0.375 to 0.375
Outputs:
- updated: float32 [8, 5, 128, 128, 128], P('group', None, 'tile')
The draws below stay inside these ranges and needn't reach their ends.
Inputs may be any that keep to these rules, and one draw needn't show every extreme that they name: `neighbours`: for each column the nine entries name the cells of its 3 x 3 neighbourhood, each once, in one of eight rotated or mirrored orders; cells are numbered in the tile extended by one cell on every side, row by row with 130 cells a row.
All inputs are finite; a program needn't handle non-finite values.
Results may differ from the reference program's by a relative error of at most 0.0016.
Values may be sent and summed in bfloat16 or wider, within the bound.
A program may use at most 128 MiB of HBM per device.

```python
import math
import jax
import jax.numpy as jnp
from jax import lax

LEV = 8
F = 5
HID = 256
TILE_ROWS = 8
CX = 128
CY = 128
TILES = 128
C = 40
FEAT = 360


def draw_neighbours(key, part):
    offset_a = jnp.array([-1, -1, -1, 0, 0, 0, 1, 1, 1], jnp.int32)[:, None, None, None]
    offset_b = jnp.array([-1, 0, 1, -1, 0, 1, -1, 0, 1], jnp.int32)[:, None, None, None]
    turns = jax.random.randint(key, (1, TILES, CX, CY), 0, 8).astype(jnp.int32)
    offset_b = jnp.where(turns >= 4, -offset_b, offset_b)
    quarter = turns % 4
    rot_a = jnp.where(quarter == 0, offset_a, jnp.where(quarter == 1, -offset_b, jnp.where(quarter == 2, -offset_a, offset_b)))
    rot_b = jnp.where(quarter == 0, offset_b, jnp.where(quarter == 1, offset_a, jnp.where(quarter == 2, -offset_b, -offset_a)))
    rows_i = jnp.arange(CX, dtype=jnp.int32)[None, None, :, None]
    cols_j = jnp.arange(CY, dtype=jnp.int32)[None, None, None, :]
    return ((rows_i + 1 + rot_a) * (CY + 2) + cols_j + 1 + rot_b).astype(jnp.int32)


def levels(rng, shape, split, low, top_value):
    gain, own = 1.0, jax.random.fold_in(rng, 6)
    for axis_at, shards_of in split:
        heights = jnp.exp(jax.random.uniform(jax.random.fold_in(own, axis_at), (shards_of,), jnp.float32, low / len(split), top_value / len(split)))
        gain = gain * jnp.repeat(heights, shape[axis_at] // shards_of).reshape([-1 if axis == axis_at else 1 for axis in range(len(shape))])
    return gain


def centred(key, shape, deviation, limit, split=(), kind=jnp.bfloat16):
    entries = jax.random.normal(key, shape, jnp.float32) * deviation
    if len(split) > 0:
        entries = levels(key, shape, split, -0.22, 0.18) * entries
    return jnp.clip(entries, min=-limit, max=limit).astype(kind)


def setup_inputs(seed: int = 0) -> dict:
    key_of = jax.random.split(jax.random.key(seed), 9)
    state = centred(key_of[0], (LEV, F, TILES, CX, CY), 1.0, 6.0, ((0, 2), (2, 128)), jnp.float32)
    courant_x = jnp.clip(jax.random.uniform(key_of[1], (LEV,), jnp.float32, -0.35, 0.35) * levels(key_of[1], (LEV,), ((0, 2),), -0.4, 0.0), -0.35, 0.35)
    courant_y = jnp.clip(jax.random.uniform(key_of[2], (LEV,), jnp.float32, -0.35, 0.35) * levels(key_of[2], (LEV,), ((0, 2),), -0.4, 0.0), -0.35, 0.35)
    diffusion = jnp.clip(jnp.exp(jax.random.uniform(key_of[3], (F,), jnp.float32, math.log(0.02), math.log(0.07))), 0.02, 0.07)
    neighbours = draw_neighbours(jax.random.fold_in(key_of[8], 71), 0)
    w_in = centred(key_of[5], (FEAT, HID), FEAT ** -0.5, 0.3125)
    w_mid = centred(key_of[6], (HID, HID), HID ** -0.5, 0.375)
    w_out = centred(key_of[7], (HID, C), HID ** -0.5, 0.375)
    return {"state": state, "courant_x": courant_x, "courant_y": courant_y, "diffusion": diffusion, "neighbours": neighbours, "w_in": w_in, "w_mid": w_mid, "w_out": w_out}


def to_grid(blocks):
    rows_x = TILES // TILE_ROWS
    grid = blocks.reshape(LEV * F, rows_x, TILE_ROWS, CX, CY).transpose(0, 1, 3, 2, 4)
    return grid.reshape(LEV * F, rows_x * CX, TILE_ROWS * CY)


def from_grid(grid):
    rows_x = TILES // TILE_ROWS
    blocks = grid.reshape(LEV, F, rows_x, CX, TILE_ROWS, CY).transpose(0, 1, 2, 4, 3, 5)
    return blocks.reshape(LEV, F, TILES, CX, CY)


def pad_border(grid):
    wrapped = jnp.pad(grid, ((0, 0), (1, 1), (0, 0)), mode="wrap")
    return jnp.pad(wrapped, ((0, 0), (0, 0), (1, 1)))


def advance(padded, speed_x, speed_y, spread):
    center = padded[:, 1:-1, 1:-1]
    lower_x = padded[:, :-2, 1:-1]
    upper_x = padded[:, 2:, 1:-1]
    lower_y = padded[:, 1:-1, :-2]
    upper_y = padded[:, 1:-1, 2:]
    result = center - jnp.maximum(speed_x, 0.0) * (center - lower_x) - jnp.minimum(speed_x, 0.0) * (upper_x - center)
    result = result - jnp.maximum(speed_y, 0.0) * (center - lower_y) - jnp.minimum(speed_y, 0.0) * (upper_y - center)
    return result + spread * (lower_x + upper_x + lower_y + upper_y - 4.0 * center)


def physics_terms(stacked, w_in, w_mid, w_out):
    contract = (((0,), (0,)), ((), ()))
    first = jax.nn.silu(lax.dot_general(w_in, stacked, contract, preferred_element_type=jnp.float32)).astype(jnp.bfloat16)
    second = jax.nn.silu(lax.dot_general(w_mid, first, contract, preferred_element_type=jnp.float32)).astype(jnp.bfloat16)
    return lax.dot_general(w_out, second, contract, preferred_element_type=jnp.float32).astype(jnp.bfloat16)


def reference(state, courant_x, courant_y, diffusion, neighbours, w_in, w_mid, w_out):
    grid = to_grid(state)
    speed_x = jnp.repeat(courant_x, F)[:, None, None]
    speed_y = jnp.repeat(courant_y, F)[:, None, None]
    spread = jnp.tile(diffusion, LEV)[:, None, None]
    for sweep in range(2):
        grid = advance(pad_border(grid), speed_x, speed_y, spread)
    padded = pad_border(grid).astype(jnp.bfloat16)

    def tile_terms(tile_number):
        start_x = ((tile_number // TILE_ROWS) * CX).astype(jnp.int32)
        start_y = ((tile_number % TILE_ROWS) * CY).astype(jnp.int32)
        window = lax.dynamic_slice(padded, (jnp.int32(0), start_x, start_y), (LEV * F, CX + 2, CY + 2))
        flat = window.reshape(LEV * F, (CX + 2) * (CY + 2))
        index = lax.dynamic_index_in_dim(neighbours, tile_number, 1, False).reshape(9, CX * CY)
        stacked = jnp.take(flat, index, axis=1).reshape(LEV * F * 9, CX * CY)
        return physics_terms(stacked, w_in, w_mid, w_out)

    terms = lax.map(tile_terms, jnp.arange(TILES, dtype=jnp.int32))
    terms = terms.reshape(TILES, LEV, F, CX, CY).transpose(1, 2, 0, 3, 4)
    return from_grid(grid) + terms.astype(jnp.float32)
```

```python
import jax
import jax.numpy as jnp
import numpy as np
from jax import lax
from jax.experimental import pallas as pl
from jax.experimental.pallas import tpu as pltpu
from jax.sharding import PartitionSpec as P

MESH = pl.DeviceIdType.MESH
F32, BF16 = jnp.float32, jnp.bfloat16
TILE_ROWS = 8
CH = 20
STRIPS = 4
PACK = STRIPS * CH
SLOTS = 18
SENDS = SLOTS // 2
STEPS = 8
KIN = 9 * 48


def feature_rows():
    table = np.full((2, STRIPS, 1, KIN), -1, np.int32)
    lead = {0: (0, 0, 16), 1: (-4, 4, 16), 2: (8, 0, 12), 3: (4, 0, 16)}
    rest = {0: (16, 0, 4), 1: (12, 0, 8), 2: (-8, 8, 16), 3: (-12, 12, 16)}
    for share in range(2):
        for strip in range(STRIPS):
            for slot, owner, (add, low, high) in (
                (0, share, lead[strip]),
                (1, 1 - share, lead[3 - strip]),
                (2, share, rest[strip]),
                (2, 1 - share, rest[3 - strip]),
            ):
                for s in range(low, high):
                    for k in range(9):
                        table[share, strip, 0, 48 * k + 16 * slot + s] = (CH * owner + s + add) * 9 + k
    return table


def kernel(
    state, speed_x, speed_y, spread, near, w_in, w_mid, w_out, table, out,
    xv, s0, s1, coef, edge, from_west, from_east, side, strips, moved_own, moved_sent, packs, arrived,
    z_own, z_sent, z_packs, z_arrived, shifted, masks, xs, ys, v_in, v_mid, v_out, w1, w2, w3, nb, tv,
    t_send, t_arrived, result,
    load_sem, pack_send, pack_recv, z_sem, t_ssem, t_rsem, halo_send, halo_recv, out_sem,
):
    tile = lax.axis_index("tile")
    g = lax.axis_index("group")
    tiles = lax.axis_size("tile")
    ty = lax.rem(tile, TILE_ROWS)
    west = (lax.rem(tile + tiles - 1, tiles), g)
    east = (lax.rem(tile + 1, tiles), g)
    north = (lax.rem(tile + tiles - TILE_ROWS, tiles), g)
    south = (lax.rem(tile + TILE_ROWS, tiles), g)
    partner = (tile, 1 - g)
    own, sent = g, 1 - g
    d_own, d_sent = 2 * own - 1, 2 * sent - 1

    def remote(src, dst, send_sem, recv_sem, device):
        return pltpu.make_async_remote_copy(
            src_ref=src, dst_ref=dst, send_sem=send_sem, recv_sem=recv_sem, device_id=device, device_id_type=MESH
        )

    loads = [
        pltpu.make_async_copy(state, xv, load_sem.at[0]),
        pltpu.make_async_copy(w_in, v_in, load_sem.at[1]),
        pltpu.make_async_copy(w_mid, v_mid, load_sem.at[2]),
        pltpu.make_async_copy(w_out, v_out, load_sem.at[3]),
        pltpu.make_async_copy(
            near.at[0:2, pl.ds(pl.multiple_of(64 * g, 64), 64)], nb, load_sem.at[4]
        ),
        pltpu.make_async_copy(table.at[g], tv, load_sem.at[5]),
    ]
    for load in loads:
        load.start()
    barrier = pltpu.get_barrier_semaphore()
    for device in (west, east, north, south, partner):
        pl.semaphore_signal(barrier, inc=1, device_id=device, device_id_type=MESH)

    chan = lax.broadcasted_iota(jnp.int32, (CH, 128), 0)
    ax = jnp.zeros((CH, 128), F32)
    ay = jnp.zeros((CH, 128), F32)
    nu = jnp.zeros((CH, 128), F32)
    for level in range(4):
        ax = jnp.where(chan // 5 == level, speed_x[level], ax)
        ay = jnp.where(chan // 5 == level, speed_y[level], ay)
    for field in range(5):
        nu = jnp.where(chan % 5 == field, spread[field], nu)
    px, mx = jnp.maximum(ax, 0.0), jnp.minimum(ax, 0.0)
    py, my = jnp.maximum(ay, 0.0), jnp.minimum(ay, 0.0)
    coef[0] = 1.0 - px + mx - py + my - 4.0 * nu
    coef[1] = px + nu
    coef[2] = nu - mx
    coef[3] = py + nu
    coef[4] = nu - my

    lane = lax.broadcasted_iota(jnp.int32, (CH, 128), 1)
    cell = lane % 8

    def substep(center, up, down, left, right):
        return center * coef[0] + up * coef[1] + down * coef[2] + left * coef[3] + right * coef[4]

    def advance_row(src, index):
        center = src[index]
        return substep(
            center, src[index - 1], src[index + 1], pltpu.roll(center, 1, 1), pltpu.roll(center, 127, 1)
        )

    loads[0].wait()
    flat = xv.reshape(CH * 128, 128)

    def spread_rows(i, edges):
        found = []
        for strip in range(8):
            row = flat[pl.ds(16 * strip + i, CH, stride=128), :]
            s0[3 + 16 * strip + i] = row
            found.append(jnp.where(lane // 8 == i, pltpu.roll(row, 8 * i + 4, 1), edges[strip]))
        return tuple(found)

    edges = lax.fori_loop(0, 16, spread_rows, tuple(jnp.zeros((CH, 128), F32) for _ in range(8)))
    for strip in range(8):
        edge[strip] = edges[strip]
    pl.semaphore_wait(barrier, 5)
    to_east = remote(edge, from_west, halo_send.at[0], halo_recv.at[0], east)
    to_west = remote(edge, from_east, halo_send.at[1], halo_recv.at[1], west)
    to_south = remote(s0.at[pl.ds(128, 3)], s0.at[pl.ds(0, 3)], halo_send.at[2], halo_recv.at[2], south)
    to_north = remote(s0.at[pl.ds(3, 3)], s0.at[pl.ds(131, 3)], halo_send.at[3], halo_recv.at[3], north)
    to_east.start()
    to_west.start()
    to_south.start()
    to_north.start()

    def first_rows(start):
        def body(n, carry):
            for u in range(5):
                index = start + 5 * n + u
                s1[index] = advance_row(s0, index)
            return carry

        lax.fori_loop(0, 13, body, 0)

    def pack_of(half, slot, order):
        place = 15 * (1 - half) + (2 * half - 1) * (slot - 1)
        return jnp.concatenate(
            [advance_row(s1, 3 + 64 * half + 16 * strip + place) for strip in order], axis=0
        )

    def pack_copy(s):
        return remote(
            packs.at[pl.ds(2 * s, 2)], arrived.at[pl.ds(2 * s, 2)], pack_send.at[s], pack_recv.at[s], partner
        )

    def send_packs(s, carry):
        for u in range(2):
            value = pack_of(sent, 2 * s + u, (3, 2, 1, 0))
            moved_sent[2 * s + u] = value
            packs[2 * s + u] = value.astype(BF16)
        pack_copy(s).start()
        return carry

    def keep_packs(s, carry):
        for u in range(2):
            moved_own[2 * s + u] = pack_of(own, 2 * s + u, (0, 1, 2, 3))
        return carry

    first_rows(3 + 1 + 61 * sent)
    lax.fori_loop(0, 7, send_packs, 0)

    out_west = cell < jnp.where(ty == 0, 4, 0)
    out_east = cell >= jnp.where(ty == TILE_ROWS - 1, 4, 8)
    to_east.wait()
    to_west.wait()
    for strip in range(8):
        here = edge[strip]
        side[strip + 1, 0] = jnp.where(out_west, 0.0, jnp.where(cell < 4, from_west[strip], here))
        side[strip + 1, 1] = jnp.where(out_east, 0.0, jnp.where(cell < 4, here, from_east[strip]))
    side_south = remote(side.at[8], side.at[0], halo_send.at[4], halo_recv.at[4], south)
    side_north = remote(side.at[1], side.at[9], halo_send.at[5], halo_recv.at[5], north)
    side_south.start()
    side_north.start()

    first_rows(3 + 1 + 61 * own)
    lax.fori_loop(0, 7, keep_packs, 0)

    for load in loads[1:]:
        load.wait()
    source = lax.broadcasted_iota(jnp.int32, (360, KIN), 0)
    for strip in range(STRIPS):
        pick = jnp.where(source == tv[strip], 0.5, 0.0).astype(BF16)
        w1[strip] = lax.dot_general(
            v_in[...], pick, (((0,), (0,)), ((), ())), preferred_element_type=F32
        ).astype(BF16)
    eye = jnp.where(
        lax.broadcasted_iota(jnp.int32, (256, 256), 0) == lax.broadcasted_iota(jnp.int32, (256, 256), 1), 0.5, 0.0
    ).astype(BF16)
    w2[...] = lax.dot_general(
        v_mid[...], eye, (((0,), (0,)), ((), ())), preferred_element_type=F32
    ).astype(BF16)
    place_out = lax.broadcasted_iota(jnp.int32, (PACK, 40), 0)
    chan_out = lax.broadcasted_iota(jnp.int32, (PACK, 40), 1)
    for strip in range(STRIPS):
        for part, at, owner in ((0, strip, g), (1, 3 - strip, 1 - g)):
            c = place_out - CH * at
            pick = jnp.where(
                (c >= 0) & (c < CH) & (chan_out == c + CH * owner), 1.0, 0.0
            ).astype(BF16)
            w3[PACK * part : PACK * (part + 1), 256 * strip : 256 * (strip + 1)] = lax.dot_general(
                pick, v_out[...], (((1,), (1,)), ((), ())), preferred_element_type=F32
            ).astype(BF16)

    to_south.wait()
    to_north.wait()
    for index in (1, 2, 3, 130, 131, 132):
        s1[index] = advance_row(s0, index)
    lax.fori_loop(7, 9, send_packs, 0)

    side_south.wait()
    side_north.wait()
    now = [[side[n, which] for n in range(10)] for which in range(2)]
    for sweep in range(2):
        later = []
        for which in range(2):
            cur = now[which]
            down8 = [pltpu.roll(v, 8, 1) for v in cur]
            up8 = [pltpu.roll(v, 120, 1) for v in cur]
            new = []
            for n in range(10):
                upper = jnp.where(lane < 8, down8[max(n - 1, 0)], down8[n])
                lower = jnp.where(lane >= 120, up8[min(n + 1, 9)], up8[n])
                value = substep(cur[n], upper, lower, pltpu.roll(cur[n], 1, 1), pltpu.roll(cur[n], 127, 1))
                new.append(jnp.where(out_east if which else out_west, 0.0, value))
            later.append(new)
        now = later
    for n in range(10):
        w, e = now[0][n], now[1][n]
        strips[n] = jnp.where(
            cell < 4, e, jnp.where(cell < 6, w, jnp.where(cell == 6, pltpu.roll(e, 2, 1), pltpu.roll(w, 4, 1)))
        )
    for k in range(3):
        at = 4 * sent + 1 + (k - 1) * d_sent
        value = jnp.concatenate([strips[at + q] for q in (3, 2, 1, 0)], axis=0)
        z_sent[k] = value
        z_packs[k] = value.astype(BF16)
    z_copy = remote(z_packs, z_arrived, z_sem.at[0], z_sem.at[1], partner)
    z_copy.start()
    for k in range(3):
        at = 4 * own + 1 + (k - 1) * d_own
        z_own[k] = jnp.concatenate([strips[at + q] for q in range(4)], axis=0)
    lax.fori_loop(7, 9, keep_packs, 0)

    lane1 = lax.broadcasted_iota(jnp.int32, (1, 128), 1)

    def order_masks(m, carry):
        place = 15 * (1 - own) + d_own * m
        flips = [[], [], []]
        for q in range(STRIPS):
            row = 16 * q + place
            centre = (64 * g + row + 1) * 130 + lane1 + 1
            first = nb[0, pl.ds(row, 1), :] - centre
            second = nb[1, pl.ds(row, 1), :] - centre
            flips[0].append(jnp.where(first > 0, 1.0, 0.0))
            flips[1].append(jnp.where((first == -129) | (first == 131), 1.0, 0.0))
            flips[2].append(jnp.where(second * second == 1, 1.0, 0.0))
        for kind in range(3):
            wide = [jnp.broadcast_to(v, (CH, 128)) for v in flips[kind]]
            masks[0, m, kind] = jnp.concatenate(wide, axis=0).astype(BF16)
            masks[1, m, kind] = jnp.concatenate(wide[::-1], axis=0).astype(BF16)
        return carry

    lax.fori_loop(0, 16, order_masks, 0)

    wide_lane = lax.broadcasted_iota(jnp.int32, (PACK, 128), 1)

    def fix_edges(value, z, place):
        return jnp.where((wide_lane < 2) | (wide_lane >= 126), pltpu.roll(z, 124 - 8 * place, 1), value)

    def ingest(slot):
        place = lax.rem(15 * (1 - own) + d_own * (slot - 1) + 16, 16)
        zi = (slot + 16) // 17 + slot // 17
        for which in range(2):
            if which == 0:
                value, z = moved_own[slot], z_own[zi]
            else:
                value, z = arrived[slot].astype(F32), z_arrived[zi].astype(F32)
            value = fix_edges(value, z, place)
            if which == 0:
                moved_own[slot] = value
            ends = pltpu.roll(z, 121 - 8 * place, 1)
            shifted[which, slot, 0] = jnp.where(wide_lane == 0, ends, pltpu.roll(value, 1, 1)).astype(BF16)
            shifted[which, slot, 1] = value.astype(BF16)
            shifted[which, slot, 2] = jnp.where(wide_lane == 127, ends, pltpu.roll(value, 127, 1)).astype(BF16)

    sub = lax.broadcasted_iota(jnp.int32, (16, 128), 0)

    def pick_neighbours(slot, u):
        cols = slice(128 * u, 128 * (u + 1))
        tails = {}
        for which in range(2):
            for t in range(5):
                rows = slice(16 * t, 16 * (t + 1))
                flip_a, flip_b, turn = (masks[which, slot - 1, kind, rows, :] > 0.5 for kind in range(3))
                a = [[shifted[which, slot + d_own * da, b, rows, :] for b in range(3)] for da in (-1, 0, 1)]
                a = [
                    [jnp.where(flip_a, a[2][b], a[0][b]) for b in range(3)],
                    a[1],
                    [jnp.where(flip_a, a[0][b], a[2][b]) for b in range(3)],
                ]
                a = [[jnp.where(flip_b, r[2], r[0]), r[1], jnp.where(flip_b, r[0], r[2])] for r in a]
                for i in range(3):
                    for j in range(3):
                        k = 3 * i + j
                        value = a[i][j] if i == j else jnp.where(turn, a[j][i], a[i][j])
                        strip = {0: 0, 1: 1, 3: 2, 4: 3}.get(t)
                        if strip is not None:
                            q = strip if which == 0 else 3 - strip
                            xs[q, 48 * k + 16 * which : 48 * k + 16 * which + 16, cols] = value
                        if t in (1, 2, 3):
                            tails[which, t, k] = value
        for k in range(9):
            at = slice(48 * k + 32, 48 * k + 48)
            low = sub < 8
            xs[0, at, cols] = jnp.where(low, tails[0, 1, k], tails[1, 3, k])
            xs[1, at, cols] = jnp.where(low, tails[0, 2, k], tails[1, 2, k])
            xs[2, at, cols] = jnp.where(low, tails[1, 2, k], tails[0, 2, k])
            xs[3, at, cols] = jnp.where(low, tails[1, 1, k], tails[0, 3, k])

    def silu_of_double(h):
        return h + h * jnp.tanh(h)

    def store_rows(value, half, place, order):
        for p, q in enumerate(order):
            flat_out[pl.ds(64 * half + 16 * q + place, CH, stride=128), :] = value[CH * p : CH * (p + 1)]

    flat_out = result.reshape(CH * 128, 128)

    def t_copy(t):
        return remote(t_send.at[t], t_arrived.at[t], t_ssem.at[t], t_rsem.at[t], partner)

    z_copy.wait()
    pack_copy(0).wait_recv()
    ingest(0)
    ingest(1)

    def physics(t, carry):
        pack_copy(t + 1).wait_recv()
        ingest(2 * t + 2)
        ingest(2 * t + 3)
        for u in range(2):
            pick_neighbours(2 * t + 1 + u, u)
        for q in range(STRIPS):
            first = silu_of_double(jnp.dot(w1[q], xs[q], preferred_element_type=F32)).astype(BF16)
            second = silu_of_double(jnp.dot(w2[...], first, preferred_element_type=F32)).astype(BF16)
            ys[256 * q : 256 * (q + 1), :] = second
        tendency = jnp.dot(w3[...], ys[...], preferred_element_type=F32).astype(BF16)
        for u in range(2):
            t_send[t, u] = tendency[PACK:, 128 * u : 128 * (u + 1)]
        t_copy(t).start()
        for u in range(2):
            place = 15 * (1 - own) + d_own * (2 * t + u)
            value = moved_own[2 * t + 1 + u] + tendency[:PACK, 128 * u : 128 * (u + 1)].astype(F32)
            store_rows(value, own, place, (0, 1, 2, 3))
        return carry

    lax.fori_loop(0, STEPS, physics, 0)

    def finish(t, carry):
        t_copy(t).wait_recv()
        for u in range(2):
            place = 15 * (1 - sent) + d_sent * (2 * t + u)
            value = fix_edges(moved_sent[2 * t + 1 + u], z_sent[1], place) + t_arrived[t, u].astype(F32)
            store_rows(value, sent, place, (3, 2, 1, 0))
        return carry

    lax.fori_loop(0, STEPS, finish, 0)
    store = pltpu.make_async_copy(result, out, out_sem)
    store.start()
    for s in range(SENDS):
        pack_copy(s).wait_send()
    for t in range(STEPS):
        t_copy(t).wait_send()
    store.wait()


def shards(state, courant_x, courant_y, diffusion, neighbours, w_in, w_mid, w_out):
    levels, fields, single, cells_x, cells_y = state.shape
    chans = levels * fields
    anywhere = pl.BlockSpec(memory_space=pl.ANY)
    scalars = pl.BlockSpec(memory_space=pltpu.SMEM)
    vmem = pltpu.VMEM
    dma = pltpu.SemaphoreType.DMA
    updated = pl.pallas_call(
        kernel,
        out_shape=jax.ShapeDtypeStruct((chans, cells_x, cells_y), F32),
        in_specs=[anywhere, scalars, scalars, scalars, anywhere, anywhere, anywhere, anywhere, anywhere],
        out_specs=anywhere,
        scratch_shapes=[
            vmem((CH, 128, 128), F32),
            vmem((134, CH, 128), F32),
            vmem((134, CH, 128), F32),
            vmem((5, CH, 128), F32),
            vmem((8, CH, 128), F32),
            vmem((8, CH, 128), F32),
            vmem((8, CH, 128), F32),
            vmem((10, 2, CH, 128), F32),
            vmem((10, CH, 128), F32),
            vmem((SLOTS, PACK, 128), F32),
            vmem((SLOTS, PACK, 128), F32),
            vmem((SLOTS, PACK, 128), BF16),
            vmem((SLOTS, PACK, 128), BF16),
            vmem((3, PACK, 128), F32),
            vmem((3, PACK, 128), F32),
            vmem((3, PACK, 128), BF16),
            vmem((3, PACK, 128), BF16),
            vmem((2, SLOTS, 3, PACK, 128), BF16),
            vmem((2, 16, 3, PACK, 128), BF16),
            vmem((STRIPS, KIN, 256), BF16),
            vmem((STRIPS * 256, 256), BF16),
            vmem((360, 256), BF16),
            vmem((256, 256), BF16),
            vmem((256, 40), BF16),
            vmem((STRIPS, 256, KIN), BF16),
            vmem((256, 256), BF16),
            vmem((2 * PACK, STRIPS * 256), BF16),
            vmem((2, 64, 128), jnp.int32),
            vmem((STRIPS, 1, KIN), jnp.int32),
            vmem((STEPS, 2, PACK, 128), BF16),
            vmem((STEPS, 2, PACK, 128), BF16),
            vmem((CH, 128, 128), F32),
            dma((6,)),
            dma((SENDS,)),
            dma((SENDS,)),
            dma((2,)),
            dma((STEPS,)),
            dma((STEPS,)),
            dma((6,)),
            dma((6,)),
            dma,
        ],
        compiler_params=pltpu.CompilerParams(
            collective_id=0, has_side_effects=True, vmem_limit_bytes=48 * 1024 * 1024
        ),
    )(
        state.reshape(chans, cells_x, cells_y),
        courant_x,
        courant_y,
        diffusion,
        neighbours.reshape(9, cells_x, cells_y),
        w_in,
        w_mid,
        w_out,
        jnp.asarray(feature_rows()),
    )
    return updated.reshape(levels, fields, single, cells_x, cells_y)


def solution(mesh):
    return jax.shard_map(
        shards,
        mesh=mesh,
        in_specs=(
            P("group", None, "tile", None, None),
            P("group"),
            P("group"),
            P(),
            P(None, "tile", None, None),
            P(),
            P(),
            P(),
        ),
        out_specs=P("group", None, "tile", None, None),
        check_vma=False,
    )
```

```python
import jax
import jax.numpy as jnp
import numpy as np
from jax import lax
from jax.experimental import pallas as pl
from jax.experimental.pallas import tpu as pltpu
from jax.sharding import PartitionSpec as P

MESH = pl.DeviceIdType.MESH
F32, BF16 = jnp.float32, jnp.bfloat16
TILE_ROWS = 8
CH = 20
STRIPS = 4
PACK = STRIPS * CH
SLOTS = 18
SENDS = SLOTS // 2
STEPS = 8
KIN = 9 * 48


def feature_rows():
    table = np.full((2, STRIPS, 1, KIN), -1, np.int32)
    lead = {0: (0, 0, 16), 1: (-4, 4, 16), 2: (8, 0, 12), 3: (4, 0, 16)}
    rest = {0: (16, 0, 4), 1: (12, 0, 8), 2: (-8, 8, 16), 3: (-12, 12, 16)}
    for share in range(2):
        for strip in range(STRIPS):
            for slot, owner, (add, low, high) in (
                (0, share, lead[strip]),
                (1, 1 - share, lead[3 - strip]),
                (2, share, rest[strip]),
                (2, 1 - share, rest[3 - strip]),
            ):
                for s in range(low, high):
                    for k in range(9):
                        table[share, strip, 0, 48 * k + 16 * slot + s] = (CH * owner + s + add) * 9 + k
    return table


def kernel(
    state, speed_x, speed_y, spread, near, w_in, w_mid, w_out, table, out,
    xv, s0, s1, coef, edge, from_west, from_east, side, strips, moved_own, moved_sent, packs, arrived,
    z_own, z_sent, z_packs, z_arrived, shifted, masks, xs_even, xs_odd, ys, v_in, v_mid, v_out, w1, w2, w3, nb, tv,
    t_send, t_arrived,
    state_sem, load_sem, pack_send, pack_recv, z_ssem, z_rsem, t_ssem, t_rsem, halo_send, halo_recv,
):
    tile = lax.axis_index("tile")
    g = lax.axis_index("group")
    tiles = lax.axis_size("tile")
    ty = lax.rem(tile, TILE_ROWS)
    west = (lax.rem(tile + tiles - 1, tiles), g)
    east = (lax.rem(tile + 1, tiles), g)
    north = (lax.rem(tile + tiles - TILE_ROWS, tiles), g)
    south = (lax.rem(tile + TILE_ROWS, tiles), g)
    partner = (tile, 1 - g)
    own, sent = g, 1 - g
    d_own, d_sent = 2 * own - 1, 2 * sent - 1

    def remote(src, dst, send_sem, recv_sem, device):
        return pltpu.make_async_remote_copy(
            src_ref=src, dst_ref=dst, send_sem=send_sem, recv_sem=recv_sem, device_id=device, device_id_type=MESH
        )

    loads = [
        pltpu.make_async_copy(w_in, v_in, load_sem.at[1]),
        pltpu.make_async_copy(w_mid, v_mid, load_sem.at[2]),
        pltpu.make_async_copy(w_out, v_out, load_sem.at[3]),
        pltpu.make_async_copy(
            near.at[0:2, pl.ds(pl.multiple_of(64 * g, 64), 64)], nb, load_sem.at[4]
        ),
        pltpu.make_async_copy(table.at[g], tv, load_sem.at[5]),
    ]
    def state_load(n):
        rows = pl.ds(pl.multiple_of(16 * n, 16), 16)
        return pltpu.make_async_copy(state.at[:, rows], xv.at[:, rows], state_sem.at[n])

    for n in range(8):
        state_load(n).start()
    for load in loads:
        load.start()
    barrier = pltpu.get_barrier_semaphore()
    for device in (north, south, partner):
        pl.semaphore_signal(barrier, inc=1, device_id=device, device_id_type=MESH)

    @pl.when(ty > 0)
    def _():
        pl.semaphore_signal(barrier, inc=1, device_id=west, device_id_type=MESH)

    @pl.when(ty < TILE_ROWS - 1)
    def _():
        pl.semaphore_signal(barrier, inc=1, device_id=east, device_id_type=MESH)

    chan = lax.broadcasted_iota(jnp.int32, (CH, 128), 0)
    ax = jnp.zeros((CH, 128), F32)
    ay = jnp.zeros((CH, 128), F32)
    nu = jnp.zeros((CH, 128), F32)
    for level in range(4):
        ax = jnp.where(chan // 5 == level, speed_x[level], ax)
        ay = jnp.where(chan // 5 == level, speed_y[level], ay)
    for field in range(5):
        nu = jnp.where(chan % 5 == field, spread[field], nu)
    px, mx = jnp.maximum(ax, 0.0), jnp.minimum(ax, 0.0)
    py, my = jnp.maximum(ay, 0.0), jnp.minimum(ay, 0.0)
    coef[0] = 1.0 - px + mx - py + my - 4.0 * nu
    coef[1] = px + nu
    coef[2] = nu - mx
    coef[3] = py + nu
    coef[4] = nu - my

    lane = lax.broadcasted_iota(jnp.int32, (CH, 128), 1)
    cell = lane % 8

    def substep(center, up, down, left, right):
        return center * coef[0] + up * coef[1] + down * coef[2] + left * coef[3] + right * coef[4]

    def advance_row(src, index):
        center = src[index]
        return substep(
            center, src[index - 1], src[index + 1], pltpu.roll(center, 1, 1), pltpu.roll(center, 127, 1)
        )

    flat = xv.reshape(CH * 128, 128)

    def spread_rows(strip, carry):
        state_load(strip).wait()
        edges = jnp.zeros((CH, 128), F32)
        for i in range(16):
            row = flat[pl.ds(16 * strip + i, CH, stride=128), :]
            s0[3 + 16 * strip + i] = row
            edges = jnp.where(lane // 8 == i, pltpu.roll(row, (8 * i + 4) % 128, 1), edges)
        edge[strip] = edges
        return carry

    lax.fori_loop(0, 8, spread_rows, 0)
    pl.semaphore_wait(barrier, 5 - jnp.where(ty == 0, 1, 0) - jnp.where(ty == TILE_ROWS - 1, 1, 0))
    to_east = remote(edge, from_west, halo_send.at[0], halo_recv.at[0], east)
    to_west = remote(edge, from_east, halo_send.at[1], halo_recv.at[1], west)
    to_south = remote(s0.at[pl.ds(128, 3)], s0.at[pl.ds(0, 3)], halo_send.at[2], halo_recv.at[2], south)
    to_north = remote(s0.at[pl.ds(3, 3)], s0.at[pl.ds(131, 3)], halo_send.at[3], halo_recv.at[3], north)

    @pl.when(ty < TILE_ROWS - 1)
    def _():
        to_east.start()

    @pl.when(ty > 0)
    def _():
        to_west.start()

    to_south.start()
    to_north.start()

    def first_rows(start):
        def body(n, carry):
            for u in range(5):
                index = start + 5 * n + u
                s1[index] = advance_row(s0, index)
            return carry

        lax.fori_loop(0, 13, body, 0)

    def pack_of(half, slot, order):
        place = 15 * (1 - half) + (2 * half - 1) * (slot - 1)
        return jnp.concatenate(
            [advance_row(s1, 3 + 64 * half + 16 * strip + place) for strip in order], axis=0
        )

    def pack_copy(s):
        return remote(
            packs.at[pl.ds(2 * s, 2)], arrived.at[pl.ds(2 * s, 2)], pack_send.at[s], pack_recv.at[s], partner
        )

    def send_packs(s, carry):
        for u in range(2):
            value = pack_of(sent, 2 * s + u, (3, 2, 1, 0))
            moved_sent[2 * s + u] = value
            packs[2 * s + u] = value.astype(BF16)
        pack_copy(s).start()
        return carry

    def keep_packs(s, carry):
        for u in range(2):
            moved_own[2 * s + u] = pack_of(own, 2 * s + u, (0, 1, 2, 3))
        return carry

    first_rows(3 + 1 + 61 * sent)
    lax.fori_loop(0, 7, send_packs, 0)

    out_west = cell < jnp.where(ty == 0, 4, 0)
    out_east = cell >= jnp.where(ty == TILE_ROWS - 1, 4, 8)
    @pl.when(ty < TILE_ROWS - 1)
    def _():
        to_east.wait_send()
        to_west.wait_recv()

    @pl.when(ty > 0)
    def _():
        to_west.wait_send()
        to_east.wait_recv()

    for strip in range(8):
        here = edge[strip]
        side[strip + 1, 0] = jnp.where(out_west, 0.0, jnp.where(cell < 4, from_west[strip], here))
        side[strip + 1, 1] = jnp.where(out_east, 0.0, jnp.where(cell < 4, here, from_east[strip]))
    side_south = remote(side.at[8], side.at[0], halo_send.at[4], halo_recv.at[4], south)
    side_north = remote(side.at[1], side.at[9], halo_send.at[5], halo_recv.at[5], north)
    side_south.start()
    side_north.start()

    def sides(group, which):
        now = [side[n, which] for n in group]
        last = len(now) - 1
        for sweep in range(2):
            down8 = [pltpu.roll(v, 8, 1) for v in now]
            up8 = [pltpu.roll(v, 120, 1) for v in now]
            later = []
            for n, cur in enumerate(now):
                upper = jnp.where(lane < 8, down8[max(n - 1, 0)], down8[n])
                lower = jnp.where(lane >= 120, up8[min(n + 1, last)], up8[n])
                value = substep(cur, upper, lower, pltpu.roll(cur, 1, 1), pltpu.roll(cur, 127, 1))
                later.append(jnp.where(out_east if which else out_west, 0.0, value))
            now = later
        return now

    def edge_values(group):
        return [
            jnp.where(
                cell < 4, e, jnp.where(cell < 6, w, jnp.where(cell == 6, pltpu.roll(e, 2, 1), pltpu.roll(w, 4, 1)))
            )
            for w, e in zip(sides(group, 0), sides(group, 1), strict=True)
        ]

    def keep_edges(k):
        shift = (0 if k in (1, 2) else 1 if k == 3 else -1)
        at = 4 * sent + 1 + shift * d_sent
        value = jnp.concatenate([strips[at + q] for q in (3, 2, 1, 0)], axis=0)
        z_sent[k] = value
        z_packs[k] = value.astype(BF16)
        at = 4 * own + 1 + shift * d_own
        z_own[k] = jnp.concatenate([strips[at + q] for q in range(4)], axis=0)

    def z_copy(n):
        return remote(z_packs.at[pl.ds(2 * n, 2)], z_arrived.at[pl.ds(2 * n, 2)], z_ssem.at[n], z_rsem.at[n], partner)

    for n, value in enumerate(edge_values(range(1, 9))):
        strips[n + 1] = value
    keep_edges(0)
    keep_edges(1)
    z_copy(0).start()

    first_rows(3 + 1 + 61 * own)
    lax.fori_loop(0, 7, keep_packs, 0)

    for load in loads:
        load.wait()
    source = lax.broadcasted_iota(jnp.int32, (360, KIN), 0)
    for strip in range(STRIPS):
        pick = jnp.where(source == tv[strip], 0.5, 0.0).astype(BF16)
        w1[strip] = lax.dot_general(
            v_in[...], pick, (((0,), (0,)), ((), ())), preferred_element_type=F32
        ).astype(BF16)
    eye = jnp.where(
        lax.broadcasted_iota(jnp.int32, (256, 256), 0) == lax.broadcasted_iota(jnp.int32, (256, 256), 1), 0.5, 0.0
    ).astype(BF16)
    w2[...] = lax.dot_general(
        v_mid[...], eye, (((0,), (0,)), ((), ())), preferred_element_type=F32
    ).astype(BF16)
    place_out = lax.broadcasted_iota(jnp.int32, (PACK, 40), 0)
    chan_out = lax.broadcasted_iota(jnp.int32, (PACK, 40), 1)
    for strip in range(STRIPS):
        for part, at, owner in ((0, strip, g), (1, 3 - strip, 1 - g)):
            c = place_out - CH * at
            pick = jnp.where(
                (c >= 0) & (c < CH) & (chan_out == c + CH * owner), 1.0, 0.0
            ).astype(BF16)
            w3[PACK * part : PACK * (part + 1), 256 * strip : 256 * (strip + 1)] = lax.dot_general(
                pick, v_out[...], (((1,), (0,)), ((), ())), preferred_element_type=F32
            ).astype(BF16)

    to_south.wait()
    to_north.wait()
    for index in (1, 2, 3, 130, 131, 132):
        s1[index] = advance_row(s0, index)
    lax.fori_loop(7, 9, send_packs, 0)
    lax.fori_loop(7, 9, keep_packs, 0)

    side_south.wait()
    side_north.wait()
    first, second = edge_values((0, 1))
    strips[0] = first
    strips[1] = jnp.where(lane < 16, second, strips[1])
    second, last = edge_values((8, 9))
    strips[8] = jnp.where(lane >= 112, second, strips[8])
    strips[9] = last
    keep_edges(2)
    keep_edges(3)
    z_copy(1).start()

    lane1 = lax.broadcasted_iota(jnp.int32, (1, 128), 1)

    def order_masks(m, carry):
        place = 15 * (1 - own) + d_own * m
        flips = [[], [], []]
        for q in range(STRIPS):
            row = 16 * q + place
            centre = (64 * g + row + 1) * 130 + lane1 + 1
            first = nb[0, pl.ds(row, 1), :] - centre
            second = nb[1, pl.ds(row, 1), :] - centre
            flips[0].append(jnp.where(first > 0, 1.0, 0.0))
            flips[1].append(jnp.where((first == -129) | (first == 131), 1.0, 0.0))
            flips[2].append(jnp.where(second * second == 1, 1.0, 0.0))
        for kind in range(3):
            wide = [jnp.broadcast_to(v, (CH, 128)) for v in flips[kind]]
            masks[0, m, kind] = jnp.concatenate(wide, axis=0).astype(BF16)
            masks[1, m, kind] = jnp.concatenate(wide[::-1], axis=0).astype(BF16)
        return carry

    lax.fori_loop(0, 16, order_masks, 0)

    wide_lane = lax.broadcasted_iota(jnp.int32, (PACK, 128), 1)

    def fix_edges(value, z, place):
        return jnp.where((wide_lane < 2) | (wide_lane >= 126), pltpu.roll(z, 124 - 8 * place, 1), value)

    def ingest(slot):
        place = lax.rem(15 * (1 - own) + d_own * (slot - 1) + 16, 16)
        zi = (slot + 16) // 17 + slot // 15 + slot // 17
        for which in range(2):
            if which == 0:
                value, z = moved_own[slot], z_own[zi]
            else:
                value, z = arrived[slot].astype(F32), z_arrived[zi].astype(F32)
            value = fix_edges(value, z, place)
            if which == 0:
                moved_own[slot] = value
            ends = pltpu.roll(z, 121 - 8 * place, 1)
            shifted[which, slot, 0] = jnp.where(wide_lane == 0, ends, pltpu.roll(value, 1, 1)).astype(BF16)
            shifted[which, slot, 1] = value.astype(BF16)
            shifted[which, slot, 2] = jnp.where(wide_lane == 127, ends, pltpu.roll(value, 127, 1)).astype(BF16)

    sub = lax.broadcasted_iota(jnp.int32, (16, 128), 0)

    def pick_neighbours(slot, u, xs):
        cols = slice(128 * u, 128 * (u + 1))
        tails = {}
        for which in range(2):
            for t in range(5):
                rows = slice(16 * t, 16 * (t + 1))
                flip_a, flip_b, turn = (masks[which, slot - 1, kind, rows, :] > 0.5 for kind in range(3))
                a = [[shifted[which, slot + d_own * da, b, rows, :] for b in range(3)] for da in (-1, 0, 1)]
                a = [
                    [jnp.where(flip_a, a[2][b], a[0][b]) for b in range(3)],
                    a[1],
                    [jnp.where(flip_a, a[0][b], a[2][b]) for b in range(3)],
                ]
                a = [[jnp.where(flip_b, r[2], r[0]), r[1], jnp.where(flip_b, r[0], r[2])] for r in a]
                for i in range(3):
                    for j in range(3):
                        k = 3 * i + j
                        value = a[i][j] if i == j else jnp.where(turn, a[j][i], a[i][j])
                        strip = {0: 0, 1: 1, 3: 2, 4: 3}.get(t)
                        if strip is not None:
                            q = strip if which == 0 else 3 - strip
                            xs[q, 48 * k + 16 * which : 48 * k + 16 * which + 16, cols] = value
                        if t in (1, 2, 3):
                            tails[which, t, k] = value
        for k in range(9):
            at = slice(48 * k + 32, 48 * k + 48)
            low = sub < 8
            xs[0, at, cols] = jnp.where(low, tails[0, 1, k], tails[1, 3, k])
            xs[1, at, cols] = jnp.where(low, tails[0, 2, k], tails[1, 2, k])
            xs[2, at, cols] = jnp.where(low, tails[1, 2, k], tails[0, 2, k])
            xs[3, at, cols] = jnp.where(low, tails[1, 1, k], tails[0, 3, k])

    def silu_of_double(h):
        return h + h * jnp.tanh(h)

    def store_rows(value, half, place, order):
        for p, q in enumerate(order):
            flat_out[pl.ds(64 * half + 16 * q + place, CH, stride=128), :] = value[CH * p : CH * (p + 1)]

    flat_out = out.reshape(CH * 128, 128)

    def t_copy(t):
        return remote(t_send.at[t], t_arrived.at[t], t_ssem.at[t], t_rsem.at[t], partner)

    def network(t, xs):
        halves = [jnp.dot(w1[q], xs[q], preferred_element_type=F32) for q in range(STRIPS)]
        first = [silu_of_double(h).astype(BF16) for h in halves]
        halves = [jnp.dot(w2[...], h, preferred_element_type=F32) for h in first]
        for q in range(STRIPS):
            ys[256 * q : 256 * (q + 1), :] = silu_of_double(halves[q]).astype(BF16)
        tendency = jnp.dot(w3[...], ys[...], preferred_element_type=F32).astype(BF16)
        for u in range(2):
            t_send[t, u] = tendency[PACK:, 128 * u : 128 * (u + 1)]
        for u in range(2):
            place = 15 * (1 - own) + d_own * (2 * t + u)
            value = moved_own[2 * t + 1 + u] + tendency[:PACK, 128 * u : 128 * (u + 1)].astype(F32)
            store_rows(value, own, place, (0, 1, 2, 3))

    z_copy(0).wait_recv()
    pack_copy(0).wait_recv()
    pack_copy(1).wait_recv()
    for slot in range(4):
        ingest(slot)
    for u in range(2):
        pick_neighbours(1 + u, u, xs_even)

    def physics(p, carry):
        for odd, (here, there) in enumerate(((xs_even, xs_odd), (xs_odd, xs_even))):
            t = 2 * p + odd

            @pl.when(t < STEPS - 1)
            def _():
                pack_copy(t + 2).wait_recv()

            @pl.when(t == 5)
            def _():
                z_copy(1).wait_recv()

            ahead = jnp.minimum(t, STEPS - 2)
            ingest(2 * ahead + 4)
            ingest(2 * ahead + 5)
            for u in range(2):
                pick_neighbours(2 * ahead + 3 + u, u, there)
            network(t, here)
            t_copy(t).start()
        return carry

    lax.fori_loop(0, STEPS // 2, physics, 0)

    def finish(t, carry):
        t_copy(t).wait_recv()
        for u in range(2):
            place = 15 * (1 - sent) + d_sent * (2 * t + u)
            value = fix_edges(moved_sent[2 * t + 1 + u], z_sent[2], place) + t_arrived[t, u].astype(F32)
            store_rows(value, sent, place, (3, 2, 1, 0))
        return carry

    lax.fori_loop(0, STEPS, finish, 0)
    z_copy(0).wait_send()
    z_copy(1).wait_send()
    for s in range(SENDS):
        pack_copy(s).wait_send()
    for t in range(STEPS):
        t_copy(t).wait_send()


def shards(state, courant_x, courant_y, diffusion, neighbours, w_in, w_mid, w_out):
    levels, fields, single, cells_x, cells_y = state.shape
    chans = levels * fields
    anywhere = pl.BlockSpec(memory_space=pltpu.HBM)
    scalars = pl.BlockSpec(memory_space=pltpu.SMEM)
    vmem = pltpu.VMEM
    dma = pltpu.SemaphoreType.DMA
    updated = pl.pallas_call(
        kernel,
        out_shape=pltpu.VMEM((chans, cells_x, cells_y), F32),
        in_specs=[anywhere, scalars, scalars, scalars, anywhere, anywhere, anywhere, anywhere, anywhere],
        out_specs=pl.BlockSpec(memory_space=vmem),
        scratch_shapes=[
            vmem((CH, 128, 128), F32),
            vmem((134, CH, 128), F32),
            vmem((134, CH, 128), F32),
            vmem((5, CH, 128), F32),
            vmem((8, CH, 128), F32),
            vmem((8, CH, 128), F32),
            vmem((8, CH, 128), F32),
            vmem((10, 2, CH, 128), F32),
            vmem((10, CH, 128), F32),
            vmem((SLOTS, PACK, 128), F32),
            vmem((SLOTS, PACK, 128), F32),
            vmem((SLOTS, PACK, 128), BF16),
            vmem((SLOTS, PACK, 128), BF16),
            vmem((4, PACK, 128), F32),
            vmem((4, PACK, 128), F32),
            vmem((4, PACK, 128), BF16),
            vmem((4, PACK, 128), BF16),
            vmem((2, SLOTS, 3, PACK, 128), BF16),
            vmem((2, 16, 3, PACK, 128), BF16),
            vmem((STRIPS, KIN, 256), BF16),
            vmem((STRIPS, KIN, 256), BF16),
            vmem((STRIPS * 256, 256), BF16),
            vmem((360, 256), BF16),
            vmem((256, 256), BF16),
            vmem((40, 256), BF16),
            vmem((STRIPS, 256, KIN), BF16),
            vmem((256, 256), BF16),
            vmem((2 * PACK, STRIPS * 256), BF16),
            vmem((2, 64, 128), jnp.int32),
            vmem((STRIPS, 1, KIN), jnp.int32),
            vmem((STEPS, 2, PACK, 128), BF16),
            vmem((STEPS, 2, PACK, 128), BF16),
            dma((8,)),
            dma((6,)),
            dma((SENDS,)),
            dma((SENDS,)),
            dma((2,)),
            dma((2,)),
            dma((STEPS,)),
            dma((STEPS,)),
            dma((6,)),
            dma((6,)),
        ],
        compiler_params=pltpu.CompilerParams(
            collective_id=0, has_side_effects=True, vmem_limit_bytes=60900 * 1024
        ),
    )(
        state.reshape(chans, cells_x, cells_y),
        courant_x,
        courant_y,
        diffusion,
        neighbours.reshape(9, cells_x, cells_y),
        w_in,
        w_mid,
        w_out.T,
        jnp.asarray(feature_rows()),
    )
    return updated.reshape(levels, fields, single, cells_x, cells_y)


def solution(mesh):
    return jax.shard_map(
        shards,
        mesh=mesh,
        in_specs=(
            P("group", None, "tile", None, None),
            P("group"),
            P("group"),
            P(),
            P(None, "tile", None, None),
            P(),
            P(),
            P(),
        ),
        out_specs=P("group", None, "tile", None, None),
        check_vma=False,
    )
```

```python
import jax
import jax.numpy as jnp
import numpy as np
from jax import lax
from jax.experimental import pallas as pl
from jax.experimental.pallas import tpu as pltpu
from jax.sharding import PartitionSpec as P

MESH = pl.DeviceIdType.MESH
F32, BF16 = jnp.float32, jnp.bfloat16
TILE_ROWS = 8
CH = 20
STRIPS = 4
PACK = STRIPS * CH
SLOTS = 18
SENDS = SLOTS // 2
STEPS = 8
AHEAD = 3
KIN = 9 * 48


def feature_rows():
    table = np.full((2, STRIPS, 1, KIN), -1, np.int32)
    lead = {0: (0, 0, 16), 1: (-4, 4, 16), 2: (8, 0, 12), 3: (4, 0, 16)}
    rest = {0: (16, 0, 4), 1: (12, 0, 8), 2: (-8, 8, 16), 3: (-12, 12, 16)}
    for share in range(2):
        for strip in range(STRIPS):
            for slot, owner, (add, low, high) in (
                (0, share, lead[strip]),
                (1, 1 - share, lead[3 - strip]),
                (2, share, rest[strip]),
                (2, 1 - share, rest[3 - strip]),
            ):
                for s in range(low, high):
                    for k in range(9):
                        table[share, strip, 0, 48 * k + 16 * slot + s] = (CH * owner + s + add) * 9 + k
    return table


def kernel(
    state, speed_x, speed_y, spread, near, w_in, w_mid, w_out, table, out,
    xv, s0, s1, coef, edge, edge_out, from_west, from_east, side, strips, moved_own, moved_sent, packs, arrived,
    z_own, z_sent, z_packs, z_arrived, shifted, masks, xs_even, xs_odd, ys, v_in, v_mid, v_out, w1, w2, w3, nb, tv,
    t_send, t_arrived,
    state_sem, load_sem, pack_send, pack_recv, z_ssem, z_rsem, t_ssem, t_rsem, halo_send, halo_recv,
):
    tile = lax.axis_index("tile")
    g = lax.axis_index("group")
    tiles = lax.axis_size("tile")
    ty = lax.rem(tile, TILE_ROWS)
    west = (lax.rem(tile + tiles - 1, tiles), g)
    east = (lax.rem(tile + 1, tiles), g)
    north = (lax.rem(tile + tiles - TILE_ROWS, tiles), g)
    south = (lax.rem(tile + TILE_ROWS, tiles), g)
    partner = (tile, 1 - g)
    own, sent = g, 1 - g
    d_own, d_sent = 2 * own - 1, 2 * sent - 1

    def remote(src, dst, send_sem, recv_sem, device):
        return pltpu.make_async_remote_copy(
            src_ref=src, dst_ref=dst, send_sem=send_sem, recv_sem=recv_sem, device_id=device, device_id_type=MESH
        )

    loads = [
        pltpu.make_async_copy(w_in, v_in, load_sem.at[1]),
        pltpu.make_async_copy(w_mid, v_mid, load_sem.at[2]),
        pltpu.make_async_copy(w_out, v_out, load_sem.at[3]),
        pltpu.make_async_copy(
            near.at[0:2, pl.ds(pl.multiple_of(64 * g, 64), 64)], nb, load_sem.at[4]
        ),
        pltpu.make_async_copy(table.at[g], tv, load_sem.at[5]),
    ]
    def state_load(n):
        rows = pl.ds(pl.multiple_of(16 * n, 16), 16)
        return pltpu.make_async_copy(state.at[:, rows], xv.at[:, rows], state_sem.at[n])

    for load in loads:
        load.start()
    for n in range(8):
        state_load(n).start()
    barrier = pltpu.get_barrier_semaphore()
    for device in (north, south, partner):
        pl.semaphore_signal(barrier, inc=1, device_id=device, device_id_type=MESH)

    @pl.when(ty > 0)
    def _():
        pl.semaphore_signal(barrier, inc=1, device_id=west, device_id_type=MESH)

    @pl.when(ty < TILE_ROWS - 1)
    def _():
        pl.semaphore_signal(barrier, inc=1, device_id=east, device_id_type=MESH)

    chan = lax.broadcasted_iota(jnp.int32, (CH, 128), 0)
    ax = jnp.zeros((CH, 128), F32)
    ay = jnp.zeros((CH, 128), F32)
    nu = jnp.zeros((CH, 128), F32)
    for level in range(4):
        ax = jnp.where(chan // 5 == level, speed_x[level], ax)
        ay = jnp.where(chan // 5 == level, speed_y[level], ay)
    for field in range(5):
        nu = jnp.where(chan % 5 == field, spread[field], nu)
    px, mx = jnp.maximum(ax, 0.0), jnp.minimum(ax, 0.0)
    py, my = jnp.maximum(ay, 0.0), jnp.minimum(ay, 0.0)
    coef[0] = 1.0 - px + mx - py + my - 4.0 * nu
    coef[1] = px + nu
    coef[2] = nu - mx
    coef[3] = py + nu
    coef[4] = nu - my

    lane = lax.broadcasted_iota(jnp.int32, (CH, 128), 1)
    cell = lane % 8

    def substep(center, up, down, left, right):
        return center * coef[0] + up * coef[1] + down * coef[2] + left * coef[3] + right * coef[4]

    def advance_row(src, index):
        center = src[index]
        return substep(
            center, src[index - 1], src[index + 1], pltpu.roll(center, 1, 1), pltpu.roll(center, 127, 1)
        )

    loads[3].wait()
    lane1 = lax.broadcasted_iota(jnp.int32, (1, 128), 1)

    def order_masks(m, carry):
        place = 15 * (1 - own) + d_own * m
        flips = [[], [], []]
        for q in range(STRIPS):
            row = 16 * q + place
            centre = (64 * g + row + 1) * 130 + lane1 + 1
            first = nb[0, pl.ds(row, 1), :] - centre
            second = nb[1, pl.ds(row, 1), :] - centre
            flips[0].append(jnp.where(first > 0, 1.0, 0.0))
            flips[1].append(jnp.where((first == -129) | (first == 131), 1.0, 0.0))
            flips[2].append(jnp.where(second * second == 1, 1.0, 0.0))
        for kind in range(3):
            wide = [jnp.broadcast_to(v, (CH, 128)) for v in flips[kind]]
            masks[0, m, kind] = jnp.concatenate(wide, axis=0).astype(BF16)
            masks[1, m, kind] = jnp.concatenate(wide[::-1], axis=0).astype(BF16)
        return carry

    lax.fori_loop(0, 16, order_masks, 0)

    flat = xv.reshape(CH * 128, 128)

    def spread_rows(strip, carry):
        state_load(strip).wait()
        edges = jnp.zeros((CH, 128), F32)
        for i in range(16):
            row = flat[pl.ds(16 * strip + i, CH, stride=128), :]
            s0[3 + 16 * strip + i] = row
            edges = jnp.where(lane // 8 == i, pltpu.roll(row, (8 * i + 4) % 128, 1), edges)
        edge[strip] = edges
        return carry

    lax.fori_loop(0, 8, spread_rows, 0)
    for n in range(4):
        edge_out[0, n] = jnp.where(cell < 4, edge[n], pltpu.roll(edge[n + 4], 4, 1))
        edge_out[1, n] = jnp.where(cell < 4, pltpu.roll(edge[n + 4], 124, 1), edge[n])
    pl.semaphore_wait(barrier, 5 - jnp.where(ty == 0, 1, 0) - jnp.where(ty == TILE_ROWS - 1, 1, 0))
    to_east = remote(edge_out.at[0], from_west, halo_send.at[0], halo_recv.at[0], east)
    to_west = remote(edge_out.at[1], from_east, halo_send.at[1], halo_recv.at[1], west)
    to_south = remote(s0.at[pl.ds(128, 3)], s0.at[pl.ds(0, 3)], halo_send.at[2], halo_recv.at[2], south)
    to_north = remote(s0.at[pl.ds(3, 3)], s0.at[pl.ds(131, 3)], halo_send.at[3], halo_recv.at[3], north)

    @pl.when(ty < TILE_ROWS - 1)
    def _():
        to_east.start()

    @pl.when(ty > 0)
    def _():
        to_west.start()

    to_south.start()
    to_north.start()

    def first_rows(start):
        def body(n, carry):
            for u in range(5):
                index = start + 5 * n + u
                s1[index] = advance_row(s0, index)
            return carry

        lax.fori_loop(0, 13, body, 0)

    def pack_of(half, slot, order):
        place = 15 * (1 - half) + (2 * half - 1) * (slot - 1)
        return jnp.concatenate(
            [advance_row(s1, 3 + 64 * half + 16 * strip + place) for strip in order], axis=0
        )

    def pack_copy(s):
        return remote(
            packs.at[pl.ds(2 * s, 2)], arrived.at[pl.ds(2 * s, 2)], pack_send.at[s], pack_recv.at[s], partner
        )

    def send_packs(s, carry):
        for u in range(2):
            value = pack_of(sent, 2 * s + u, (3, 2, 1, 0))
            moved_sent[2 * s + u] = value
            packs[2 * s + u] = value.astype(BF16)
        pack_copy(s).start()
        return carry

    def keep_packs(s, carry):
        for u in range(2):
            moved_own[2 * s + u] = pack_of(own, 2 * s + u, (0, 1, 2, 3))
        return carry

    first_rows(3 + 1 + 61 * sent)
    lax.fori_loop(0, AHEAD, send_packs, 0)
    first_rows(3 + 1 + 61 * own)

    for load in loads[:3] + loads[4:]:
        load.wait()
    source = lax.broadcasted_iota(jnp.int32, (360, KIN), 0)
    for strip in range(STRIPS):
        pick = jnp.where(source == tv[strip], 0.5, 0.0).astype(BF16)
        w1[strip] = lax.dot_general(
            v_in[...], pick, (((0,), (0,)), ((), ())), preferred_element_type=F32
        ).astype(BF16)
    eye = jnp.where(
        lax.broadcasted_iota(jnp.int32, (256, 256), 0) == lax.broadcasted_iota(jnp.int32, (256, 256), 1), 0.5, 0.0
    ).astype(BF16)
    w2[...] = lax.dot_general(
        v_mid[...], eye, (((0,), (0,)), ((), ())), preferred_element_type=F32
    ).astype(BF16)
    place_out = lax.broadcasted_iota(jnp.int32, (PACK, 40), 0)
    chan_out = lax.broadcasted_iota(jnp.int32, (PACK, 40), 1)
    for strip in range(STRIPS):
        for part, at, owner in ((0, strip, g), (1, 3 - strip, 1 - g)):
            c = place_out - CH * at
            pick = jnp.where(
                (c >= 0) & (c < CH) & (chan_out == c + CH * owner), 1.0, 0.0
            ).astype(BF16)
            w3[PACK * part : PACK * (part + 1), 256 * strip : 256 * (strip + 1)] = lax.dot_general(
                pick, v_out[...], (((1,), (0,)), ((), ())), preferred_element_type=F32
            ).astype(BF16)


    out_west = cell < jnp.where(ty == 0, 4, 0)
    out_east = cell >= jnp.where(ty == TILE_ROWS - 1, 4, 8)
    @pl.when(ty < TILE_ROWS - 1)
    def _():
        to_east.wait_send()
        to_west.wait_recv()

    @pl.when(ty > 0)
    def _():
        to_west.wait_send()
        to_east.wait_recv()

    for strip in range(8):
        here = edge[strip]
        beyond_west, beyond_east = from_west[strip % 4], from_east[strip % 4]
        if strip >= 4:
            beyond_west, beyond_east = pltpu.roll(beyond_west, 124, 1), pltpu.roll(beyond_east, 4, 1)
        side[strip + 1, 0] = jnp.where(out_west, 0.0, jnp.where(cell < 4, beyond_west, here))
        side[strip + 1, 1] = jnp.where(out_east, 0.0, jnp.where(cell < 4, here, beyond_east))
    side_south = remote(side.at[8], side.at[0], halo_send.at[4], halo_recv.at[4], south)
    side_north = remote(side.at[1], side.at[9], halo_send.at[5], halo_recv.at[5], north)
    side_south.start()
    side_north.start()

    def sides(group, which):
        now = [side[n, which] for n in group]
        last = len(now) - 1
        for sweep in range(2):
            down8 = [pltpu.roll(v, 8, 1) for v in now]
            up8 = [pltpu.roll(v, 120, 1) for v in now]
            later = []
            for n, cur in enumerate(now):
                upper = jnp.where(lane < 8, down8[max(n - 1, 0)], down8[n])
                lower = jnp.where(lane >= 120, up8[min(n + 1, last)], up8[n])
                value = substep(cur, upper, lower, pltpu.roll(cur, 1, 1), pltpu.roll(cur, 127, 1))
                later.append(jnp.where(out_east if which else out_west, 0.0, value))
            now = later
        return now

    def edge_values(group):
        return [
            jnp.where(
                cell < 4, e, jnp.where(cell < 6, w, jnp.where(cell == 6, pltpu.roll(e, 2, 1), pltpu.roll(w, 4, 1)))
            )
            for w, e in zip(sides(group, 0), sides(group, 1), strict=True)
        ]

    def keep_edges(k):
        shift = (0 if k in (1, 2) else 1 if k == 3 else -1)
        at = 4 * sent + 1 + shift * d_sent
        value = jnp.concatenate([strips[at + q] for q in (3, 2, 1, 0)], axis=0)
        z_sent[k] = value
        z_packs[k] = value.astype(BF16)
        at = 4 * own + 1 + shift * d_own
        z_own[k] = jnp.concatenate([strips[at + q] for q in range(4)], axis=0)

    def z_copy(n):
        return remote(z_packs.at[pl.ds(2 * n, 2)], z_arrived.at[pl.ds(2 * n, 2)], z_ssem.at[n], z_rsem.at[n], partner)

    for n, value in enumerate(edge_values(range(1, 9))):
        strips[n + 1] = value
    keep_edges(0)
    keep_edges(1)
    z_copy(0).start()

    lax.fori_loop(AHEAD, 7, send_packs, 0)
    lax.fori_loop(0, 2, keep_packs, 0)

    wide_lane = lax.broadcasted_iota(jnp.int32, (PACK, 128), 1)

    def fix_edges(value, z, place):
        return jnp.where((wide_lane < 2) | (wide_lane >= 126), pltpu.roll(z, 124 - 8 * place, 1), value)

    def ingest(slot):
        place = lax.rem(15 * (1 - own) + d_own * (slot - 1) + 16, 16)
        zi = (slot + 16) // 17 + slot // 15 + slot // 17
        for which in range(2):
            if which == 0:
                value, z = moved_own[slot], z_own[zi]
            else:
                value, z = arrived[slot].astype(F32), z_arrived[zi].astype(F32)
            value = fix_edges(value, z, place)
            if which == 0:
                moved_own[slot] = value
            ends = pltpu.roll(z, 121 - 8 * place, 1)
            shifted[which, slot, 0] = jnp.where(wide_lane == 0, ends, pltpu.roll(value, 1, 1)).astype(BF16)
            shifted[which, slot, 1] = value.astype(BF16)
            shifted[which, slot, 2] = jnp.where(wide_lane == 127, ends, pltpu.roll(value, 127, 1)).astype(BF16)

    sub = lax.broadcasted_iota(jnp.int32, (16, 128), 0)

    def pick_neighbours(slot, u, xs):
        cols = slice(128 * u, 128 * (u + 1))
        tails = {}
        for which in range(2):
            for t in range(5):
                rows = slice(16 * t, 16 * (t + 1))
                flip_a, flip_b, turn = (masks[which, slot - 1, kind, rows, :] > 0.5 for kind in range(3))
                a = [[shifted[which, slot + d_own * da, b, rows, :] for b in range(3)] for da in (-1, 0, 1)]
                a = [
                    [jnp.where(flip_a, a[2][b], a[0][b]) for b in range(3)],
                    a[1],
                    [jnp.where(flip_a, a[0][b], a[2][b]) for b in range(3)],
                ]
                a = [[jnp.where(flip_b, r[2], r[0]), r[1], jnp.where(flip_b, r[0], r[2])] for r in a]
                for i in range(3):
                    for j in range(3):
                        k = 3 * i + j
                        value = a[i][j] if i == j else jnp.where(turn, a[j][i], a[i][j])
                        strip = {0: 0, 1: 1, 3: 2, 4: 3}.get(t)
                        if strip is not None:
                            q = strip if which == 0 else 3 - strip
                            xs[q, 48 * k + 16 * which : 48 * k + 16 * which + 16, cols] = value
                        if t in (1, 2, 3):
                            tails[which, t, k] = value
        for k in range(9):
            at = slice(48 * k + 32, 48 * k + 48)
            low = sub < 8
            xs[0, at, cols] = jnp.where(low, tails[0, 1, k], tails[1, 3, k])
            xs[1, at, cols] = jnp.where(low, tails[0, 2, k], tails[1, 2, k])
            xs[2, at, cols] = jnp.where(low, tails[1, 2, k], tails[0, 2, k])
            xs[3, at, cols] = jnp.where(low, tails[1, 1, k], tails[0, 3, k])

    def silu_of_double(h):
        return h + h * jnp.tanh(h)

    def store_rows(value, half, place, order):
        for p, q in enumerate(order):
            flat_out[pl.ds(64 * half + 16 * q + place, CH, stride=128), :] = value[CH * p : CH * (p + 1)]

    flat_out = out.reshape(CH * 128, 128)

    def t_copy(t):
        return remote(t_send.at[t], t_arrived.at[t], t_ssem.at[t], t_rsem.at[t], partner)

    def borders():
        to_south.wait()
        to_north.wait()
        for index in (1, 2, 3, 130, 131, 132):
            s1[index] = advance_row(s0, index)
        lax.fori_loop(7, 9, send_packs, 0)

        side_south.wait()
        side_north.wait()
        first, second = edge_values((0, 1))
        strips[0] = first
        strips[1] = jnp.where(lane < 16, second, strips[1])
        second, last = edge_values((8, 9))
        strips[8] = jnp.where(lane >= 112, second, strips[8])
        strips[9] = last
        keep_edges(2)
        keep_edges(3)
        z_copy(1).start()

    def network(t, xs, beside):
        halves, first = [], []
        for q in range(STRIPS):
            halves.append(jnp.dot(w1[q], xs[q], preferred_element_type=F32))
            if q == 1:
                beside[0]()
        for q in range(STRIPS):
            first.append(silu_of_double(halves[q]).astype(BF16))
            halves[q] = jnp.dot(w2[...], first[q], preferred_element_type=F32)
            if q == 1:
                beside[1]()
        beside[2]()
        for q in range(STRIPS):
            ys[256 * q : 256 * (q + 1), :] = silu_of_double(halves[q]).astype(BF16)
        tendency = jnp.dot(w3[...], ys[...], preferred_element_type=F32).astype(BF16)
        for u in range(2):
            t_send[t, u] = tendency[PACK:, 128 * u : 128 * (u + 1)]
        for u in range(2):
            place = 15 * (1 - own) + d_own * (2 * t + u)
            value = moved_own[2 * t + 1 + u] + tendency[:PACK, 128 * u : 128 * (u + 1)].astype(F32)
            store_rows(value, own, place, (0, 1, 2, 3))

    z_copy(0).wait_recv()
    pack_copy(0).wait_recv()
    pack_copy(1).wait_recv()
    for slot in range(4):
        ingest(slot)
    for u in range(2):
        pick_neighbours(1 + u, u, xs_even)

    nothing = (lambda: None,) * 3

    def beside(t, xs):
        def prepare():
            keep_packs(t + 2, 0)
            ingest(2 * t + 4)
            ingest(2 * t + 5)

        return (
            prepare,
            lambda: pick_neighbours(2 * t + 3, 0, xs),
            lambda: pick_neighbours(2 * t + 4, 1, xs),
        )

    def physics(p, carry):
        for odd, (here, there) in enumerate(((xs_even, xs_odd), (xs_odd, xs_even))):
            t = 2 * p + odd
            pack_copy(t + 2).wait_recv()
            if odd:

                @pl.when(p == 0)
                def _():
                    borders()

                @pl.when(p == 2)
                def _():
                    z_copy(1).wait_recv()

            network(t, here, beside(t, there))
            t_copy(t).start()
        return carry

    lax.fori_loop(0, STEPS // 2 - 1, physics, 0)
    pack_copy(STEPS).wait_recv()
    network(STEPS - 2, xs_even, beside(STEPS - 2, xs_odd))
    t_copy(STEPS - 2).start()
    network(STEPS - 1, xs_odd, nothing)
    t_copy(STEPS - 1).start()

    def finish(t, carry):
        t_copy(t).wait_recv()
        for u in range(2):
            place = 15 * (1 - sent) + d_sent * (2 * t + u)
            value = fix_edges(moved_sent[2 * t + 1 + u], z_sent[2], place) + t_arrived[t, u].astype(F32)
            store_rows(value, sent, place, (3, 2, 1, 0))
        return carry

    lax.fori_loop(0, STEPS, finish, 0)
    z_copy(0).wait_send()
    z_copy(1).wait_send()
    for s in range(SENDS):
        pack_copy(s).wait_send()
    for t in range(STEPS):
        t_copy(t).wait_send()


def shards(state, courant_x, courant_y, diffusion, neighbours, w_in, w_mid, w_out):
    levels, fields, single, cells_x, cells_y = state.shape
    chans = levels * fields
    anywhere = pl.BlockSpec(memory_space=pltpu.HBM)
    scalars = pl.BlockSpec(memory_space=pltpu.SMEM)
    vmem = pltpu.VMEM
    dma = pltpu.SemaphoreType.DMA
    updated = pl.pallas_call(
        kernel,
        out_shape=pltpu.VMEM((chans, cells_x, cells_y), F32),
        in_specs=[anywhere, scalars, scalars, scalars, anywhere, anywhere, anywhere, anywhere, anywhere],
        out_specs=pl.BlockSpec(memory_space=vmem),
        scratch_shapes=[
            vmem((CH, 128, 128), F32),
            vmem((134, CH, 128), F32),
            vmem((134, CH, 128), F32),
            vmem((5, CH, 128), F32),
            vmem((8, CH, 128), F32),
            vmem((2, 4, CH, 128), F32),
            vmem((4, CH, 128), F32),
            vmem((4, CH, 128), F32),
            vmem((10, 2, CH, 128), F32),
            vmem((10, CH, 128), F32),
            vmem((SLOTS, PACK, 128), F32),
            vmem((SLOTS, PACK, 128), F32),
            vmem((SLOTS, PACK, 128), BF16),
            vmem((SLOTS, PACK, 128), BF16),
            vmem((4, PACK, 128), F32),
            vmem((4, PACK, 128), F32),
            vmem((4, PACK, 128), BF16),
            vmem((4, PACK, 128), BF16),
            vmem((2, SLOTS, 3, PACK, 128), BF16),
            vmem((2, 16, 3, PACK, 128), BF16),
            vmem((STRIPS, KIN, 256), BF16),
            vmem((STRIPS, KIN, 256), BF16),
            vmem((STRIPS * 256, 256), BF16),
            vmem((360, 256), BF16),
            vmem((256, 256), BF16),
            vmem((40, 256), BF16),
            vmem((STRIPS, 256, KIN), BF16),
            vmem((256, 256), BF16),
            vmem((2 * PACK, STRIPS * 256), BF16),
            vmem((2, 64, 128), jnp.int32),
            vmem((STRIPS, 1, KIN), jnp.int32),
            vmem((STEPS, 2, PACK, 128), BF16),
            vmem((STEPS, 2, PACK, 128), BF16),
            dma((8,)),
            dma((6,)),
            dma((SENDS,)),
            dma((SENDS,)),
            dma((2,)),
            dma((2,)),
            dma((STEPS,)),
            dma((STEPS,)),
            dma((6,)),
            dma((6,)),
        ],
        compiler_params=pltpu.CompilerParams(
            collective_id=0, has_side_effects=True, vmem_limit_bytes=60900 * 1024
        ),
    )(
        state.reshape(chans, cells_x, cells_y),
        courant_x,
        courant_y,
        diffusion,
        neighbours.reshape(9, cells_x, cells_y),
        w_in,
        w_mid,
        w_out.T,
        jnp.asarray(feature_rows()),
    )
    return updated.reshape(levels, fields, single, cells_x, cells_y)


def solution(mesh):
    return jax.shard_map(
        shards,
        mesh=mesh,
        in_specs=(
            P("group", None, "tile", None, None),
            P("group"),
            P("group"),
            P(),
            P(None, "tile", None, None),
            P(),
            P(),
            P(),
        ),
        out_specs=P("group", None, "tile", None, None),
        check_vma=False,
    )
```

```python
import jax
import jax.numpy as jnp
import numpy as np
from jax import lax
from jax.experimental import pallas as pl
from jax.experimental.pallas import tpu as pltpu
from jax.sharding import PartitionSpec as P

MESH = pl.DeviceIdType.MESH
F32, BF16 = jnp.float32, jnp.bfloat16
TILE_ROWS = 8
CH = 20
STRIPS = 4
PACK = STRIPS * CH
SLOTS = 18
SENDS = SLOTS // 2
STEPS = 8
AHEAD = 3
KIN = 9 * 48


def feature_rows():
    table = np.full((2, STRIPS, 1, KIN), -1, np.int32)
    lead = {0: (0, 0, 16), 1: (-4, 4, 16), 2: (8, 0, 12), 3: (4, 0, 16)}
    rest = {0: (16, 0, 4), 1: (12, 0, 8), 2: (-8, 8, 16), 3: (-12, 12, 16)}
    for share in range(2):
        for strip in range(STRIPS):
            for slot, owner, (add, low, high) in (
                (0, share, lead[strip]),
                (1, 1 - share, lead[3 - strip]),
                (2, share, rest[strip]),
                (2, 1 - share, rest[3 - strip]),
            ):
                for s in range(low, high):
                    for k in range(9):
                        table[share, strip, 0, 48 * k + 16 * slot + s] = (CH * owner + s + add) * 9 + k
    return table


def kernel(
    state, speed_x, speed_y, spread, near, w_in, w_mid, w_out, table, out,
    xv, s0, s1, coef, edge, edge_out, from_west, from_east, side, strips, moved_own, moved_sent, packs, arrived,
    z_own, z_sent, z_packs, z_arrived, shifted, masks, xs_even, xs_odd, ys, v_in, v_mid, v_out, w1, w2, w3, nb, tv,
    t_send, t_arrived,
    state_sem, load_sem, pack_send, pack_recv, z_ssem, z_rsem, t_ssem, t_rsem, halo_send, halo_recv,
):
    tile = lax.axis_index("tile")
    g = lax.axis_index("group")
    tiles = lax.axis_size("tile")
    ty = lax.rem(tile, TILE_ROWS)
    west = (lax.rem(tile + tiles - 1, tiles), g)
    east = (lax.rem(tile + 1, tiles), g)
    north = (lax.rem(tile + tiles - TILE_ROWS, tiles), g)
    south = (lax.rem(tile + TILE_ROWS, tiles), g)
    partner = (tile, 1 - g)
    own, sent = g, 1 - g
    d_own, d_sent = 2 * own - 1, 2 * sent - 1

    def remote(src, dst, send_sem, recv_sem, device):
        return pltpu.make_async_remote_copy(
            src_ref=src, dst_ref=dst, send_sem=send_sem, recv_sem=recv_sem, device_id=device, device_id_type=MESH
        )

    loads = [
        pltpu.make_async_copy(w_in, v_in, load_sem.at[1]),
        pltpu.make_async_copy(w_mid, v_mid, load_sem.at[2]),
        pltpu.make_async_copy(w_out, v_out, load_sem.at[3]),
        pltpu.make_async_copy(
            near.at[0:2, pl.ds(pl.multiple_of(64 * g, 64), 64)], nb, load_sem.at[4]
        ),
        pltpu.make_async_copy(table.at[g], tv, load_sem.at[5]),
    ]
    def state_load(n):
        rows = pl.ds(pl.multiple_of(16 * n, 16), 16)
        return pltpu.make_async_copy(state.at[:, rows], xv.at[:, rows], state_sem.at[n])

    loads[3].start()
    for n in range(8):
        state_load(n).start()
    barrier = pltpu.get_barrier_semaphore()
    for device in (north, south, partner):
        pl.semaphore_signal(barrier, inc=1, device_id=device, device_id_type=MESH)

    @pl.when(ty > 0)
    def _():
        pl.semaphore_signal(barrier, inc=1, device_id=west, device_id_type=MESH)

    @pl.when(ty < TILE_ROWS - 1)
    def _():
        pl.semaphore_signal(barrier, inc=1, device_id=east, device_id_type=MESH)

    for load in loads[:3] + loads[4:]:
        load.start()

    chan = lax.broadcasted_iota(jnp.int32, (CH, 128), 0)
    ax = jnp.zeros((CH, 128), F32)
    ay = jnp.zeros((CH, 128), F32)
    nu = jnp.zeros((CH, 128), F32)
    for level in range(4):
        ax = jnp.where(chan // 5 == level, speed_x[level], ax)
        ay = jnp.where(chan // 5 == level, speed_y[level], ay)
    for field in range(5):
        nu = jnp.where(chan % 5 == field, spread[field], nu)
    px, mx = jnp.maximum(ax, 0.0), jnp.minimum(ax, 0.0)
    py, my = jnp.maximum(ay, 0.0), jnp.minimum(ay, 0.0)
    coef[0] = 1.0 - px + mx - py + my - 4.0 * nu
    coef[1] = px + nu
    coef[2] = nu - mx
    coef[3] = py + nu
    coef[4] = nu - my

    lane = lax.broadcasted_iota(jnp.int32, (CH, 128), 1)
    cell = lane % 8

    def substep(center, up, down, left, right):
        return center * coef[0] + up * coef[1] + down * coef[2] + left * coef[3] + right * coef[4]

    def advance_row(src, index):
        center = src[index]
        return substep(
            center, src[index - 1], src[index + 1], pltpu.roll(center, 1, 1), pltpu.roll(center, 127, 1)
        )

    loads[3].wait()
    lane1 = lax.broadcasted_iota(jnp.int32, (1, 128), 1)

    def order_masks(m, carry):
        place = 15 * (1 - own) + d_own * m
        flips = [[], [], []]
        for q in range(STRIPS):
            row = 16 * q + place
            centre = (64 * g + row + 1) * 130 + lane1 + 1
            first = nb[0, pl.ds(row, 1), :] - centre
            second = nb[1, pl.ds(row, 1), :] - centre
            flips[0].append(jnp.where(first > 0, 1.0, 0.0))
            flips[1].append(jnp.where((first == -129) | (first == 131), 1.0, 0.0))
            flips[2].append(jnp.where(second * second == 1, 1.0, 0.0))
        for kind in range(3):
            wide = [jnp.broadcast_to(v, (CH, 128)) for v in flips[kind]]
            masks[0, m, kind] = jnp.concatenate(wide, axis=0).astype(BF16)
            masks[1, m, kind] = jnp.concatenate(wide[::-1], axis=0).astype(BF16)
        return carry

    lax.fori_loop(0, 16, order_masks, 0)

    flat = xv.reshape(CH * 128, 128)

    def spread_rows(strip, carry):
        state_load(strip).wait()
        edges = jnp.zeros((CH, 128), F32)
        for i in range(16):
            row = flat[pl.ds(16 * strip + i, CH, stride=128), :]
            s0[3 + 16 * strip + i] = row
            edges = jnp.where(lane // 8 == i, pltpu.roll(row, (8 * i + 4) % 128, 1), edges)
        edge[strip] = edges
        return carry

    lax.fori_loop(0, 8, spread_rows, 0)
    for n in range(4):
        edge_out[0, n] = jnp.where(cell < 4, edge[n], pltpu.roll(edge[n + 4], 4, 1))
        edge_out[1, n] = jnp.where(cell < 4, pltpu.roll(edge[n + 4], 124, 1), edge[n])
    pl.semaphore_wait(barrier, 5 - jnp.where(ty == 0, 1, 0) - jnp.where(ty == TILE_ROWS - 1, 1, 0))
    to_east = remote(edge_out.at[0], from_west, halo_send.at[0], halo_recv.at[0], east)
    to_west = remote(edge_out.at[1], from_east, halo_send.at[1], halo_recv.at[1], west)
    to_south = remote(s0.at[pl.ds(128, 3)], s0.at[pl.ds(0, 3)], halo_send.at[2], halo_recv.at[2], south)
    to_north = remote(s0.at[pl.ds(3, 3)], s0.at[pl.ds(131, 3)], halo_send.at[3], halo_recv.at[3], north)

    @pl.when(ty < TILE_ROWS - 1)
    def _():
        to_east.start()

    @pl.when(ty > 0)
    def _():
        to_west.start()

    to_south.start()
    to_north.start()

    def first_rows(start):
        def body(n, carry):
            for u in range(5):
                index = start + 5 * n + u
                s1[index] = advance_row(s0, index)
            return carry

        lax.fori_loop(0, 13, body, 0)

    def pack_of(half, slot, order):
        place = 15 * (1 - half) + (2 * half - 1) * (slot - 1)
        return jnp.concatenate(
            [advance_row(s1, 3 + 64 * half + 16 * strip + place) for strip in order], axis=0
        )

    def pack_copy(s):
        return remote(
            packs.at[pl.ds(2 * s, 2)], arrived.at[pl.ds(2 * s, 2)], pack_send.at[s], pack_recv.at[s], partner
        )

    def send_packs(s, carry):
        for u in range(2):
            value = pack_of(sent, 2 * s + u, (3, 2, 1, 0))
            moved_sent[2 * s + u] = value
            packs[2 * s + u] = value.astype(BF16)
        pack_copy(s).start()
        return carry

    def keep_packs(s, carry):
        for u in range(2):
            moved_own[2 * s + u] = pack_of(own, 2 * s + u, (0, 1, 2, 3))
        return carry

    first_rows(3 + 1 + 61 * sent)
    lax.fori_loop(0, AHEAD, send_packs, 0)
    first_rows(3 + 1 + 61 * own)

    for load in loads[:3] + loads[4:]:
        load.wait()
    source = lax.broadcasted_iota(jnp.int32, (360, KIN), 0)
    for strip in range(STRIPS):
        pick = jnp.where(source == tv[strip], 0.5, 0.0).astype(BF16)
        w1[strip] = lax.dot_general(
            v_in[...], pick, (((0,), (0,)), ((), ())), preferred_element_type=F32
        ).astype(BF16)
    eye = jnp.where(
        lax.broadcasted_iota(jnp.int32, (256, 256), 0) == lax.broadcasted_iota(jnp.int32, (256, 256), 1), 0.5, 0.0
    ).astype(BF16)
    w2[...] = lax.dot_general(
        v_mid[...], eye, (((0,), (0,)), ((), ())), preferred_element_type=F32
    ).astype(BF16)
    place_out = lax.broadcasted_iota(jnp.int32, (PACK, 40), 0)
    chan_out = lax.broadcasted_iota(jnp.int32, (PACK, 40), 1)
    for strip in range(STRIPS):
        for part, at, owner in ((0, strip, g), (1, 3 - strip, 1 - g)):
            c = place_out - CH * at
            pick = jnp.where(
                (c >= 0) & (c < CH) & (chan_out == c + CH * owner), 1.0, 0.0
            ).astype(BF16)
            w3[PACK * part : PACK * (part + 1), 256 * strip : 256 * (strip + 1)] = lax.dot_general(
                pick, v_out[...], (((1,), (0,)), ((), ())), preferred_element_type=F32
            ).astype(BF16)


    out_west = cell < jnp.where(ty == 0, 4, 0)
    out_east = cell >= jnp.where(ty == TILE_ROWS - 1, 4, 8)
    @pl.when(ty < TILE_ROWS - 1)
    def _():
        to_east.wait_send()
        to_west.wait_recv()

    @pl.when(ty > 0)
    def _():
        to_west.wait_send()
        to_east.wait_recv()

    for strip in range(8):
        here = edge[strip]
        beyond_west, beyond_east = from_west[strip % 4], from_east[strip % 4]
        if strip >= 4:
            beyond_west, beyond_east = pltpu.roll(beyond_west, 124, 1), pltpu.roll(beyond_east, 4, 1)
        side[strip + 1, 0] = jnp.where(out_west, 0.0, jnp.where(cell < 4, beyond_west, here))
        side[strip + 1, 1] = jnp.where(out_east, 0.0, jnp.where(cell < 4, here, beyond_east))
    side_south = remote(side.at[8], side.at[0], halo_send.at[4], halo_recv.at[4], south)
    side_north = remote(side.at[1], side.at[9], halo_send.at[5], halo_recv.at[5], north)
    side_south.start()
    side_north.start()

    def sides(group, which):
        now = [side[n, which] for n in group]
        last = len(now) - 1
        for sweep in range(2):
            down8 = [pltpu.roll(v, 8, 1) for v in now]
            up8 = [pltpu.roll(v, 120, 1) for v in now]
            later = []
            for n, cur in enumerate(now):
                upper = jnp.where(lane < 8, down8[max(n - 1, 0)], down8[n])
                lower = jnp.where(lane >= 120, up8[min(n + 1, last)], up8[n])
                value = substep(cur, upper, lower, pltpu.roll(cur, 1, 1), pltpu.roll(cur, 127, 1))
                later.append(jnp.where(out_east if which else out_west, 0.0, value))
            now = later
        return now

    def edge_values(group):
        return [
            jnp.where(
                cell < 4, e, jnp.where(cell < 6, w, jnp.where(cell == 6, pltpu.roll(e, 2, 1), pltpu.roll(w, 4, 1)))
            )
            for w, e in zip(sides(group, 0), sides(group, 1), strict=True)
        ]

    def keep_edges(k):
        shift = (0 if k in (1, 2) else 1 if k == 3 else -1)
        at = 4 * sent + 1 + shift * d_sent
        value = jnp.concatenate([strips[at + q] for q in (3, 2, 1, 0)], axis=0)
        z_sent[k] = value
        z_packs[k] = value.astype(BF16)
        at = 4 * own + 1 + shift * d_own
        z_own[k] = jnp.concatenate([strips[at + q] for q in range(4)], axis=0)

    def z_copy(n):
        return remote(z_packs.at[pl.ds(2 * n, 2)], z_arrived.at[pl.ds(2 * n, 2)], z_ssem.at[n], z_rsem.at[n], partner)

    for n, value in enumerate(edge_values(range(1, 9))):
        strips[n + 1] = value
    keep_edges(0)
    keep_edges(1)
    z_copy(0).start()

    lax.fori_loop(AHEAD, 7, send_packs, 0)
    lax.fori_loop(0, 2, keep_packs, 0)

    wide_lane = lax.broadcasted_iota(jnp.int32, (PACK, 128), 1)

    def fix_edges(value, z, place):
        return jnp.where((wide_lane < 2) | (wide_lane >= 126), pltpu.roll(z, 124 - 8 * place, 1), value)

    def ingest(slot):
        place = lax.rem(15 * (1 - own) + d_own * (slot - 1) + 16, 16)
        zi = (slot + 16) // 17 + slot // 15 + slot // 17
        for which in range(2):
            if which == 0:
                value, z = moved_own[slot], z_own[zi]
            else:
                value, z = arrived[slot].astype(F32), z_arrived[zi].astype(F32)
            value = fix_edges(value, z, place)
            if which == 0:
                moved_own[slot] = value
            ends = pltpu.roll(z, 121 - 8 * place, 1)
            shifted[which, slot, 0] = jnp.where(wide_lane == 0, ends, pltpu.roll(value, 1, 1)).astype(BF16)
            shifted[which, slot, 1] = value.astype(BF16)
            shifted[which, slot, 2] = jnp.where(wide_lane == 127, ends, pltpu.roll(value, 127, 1)).astype(BF16)

    sub = lax.broadcasted_iota(jnp.int32, (16, 128), 0)

    def pick_neighbours(slot, u, xs):
        cols = slice(128 * u, 128 * (u + 1))
        tails = {}
        for which in range(2):
            for t in range(5):
                rows = slice(16 * t, 16 * (t + 1))
                flip_a, flip_b, turn = (masks[which, slot - 1, kind, rows, :] > 0.5 for kind in range(3))
                a = [[shifted[which, slot + d_own * da, b, rows, :] for b in range(3)] for da in (-1, 0, 1)]
                a = [
                    [jnp.where(flip_a, a[2][b], a[0][b]) for b in range(3)],
                    a[1],
                    [jnp.where(flip_a, a[0][b], a[2][b]) for b in range(3)],
                ]
                a = [[jnp.where(flip_b, r[2], r[0]), r[1], jnp.where(flip_b, r[0], r[2])] for r in a]
                for i in range(3):
                    for j in range(3):
                        k = 3 * i + j
                        value = a[i][j] if i == j else jnp.where(turn, a[j][i], a[i][j])
                        strip = {0: 0, 1: 1, 3: 2, 4: 3}.get(t)
                        if strip is not None:
                            q = strip if which == 0 else 3 - strip
                            xs[q, 48 * k + 16 * which : 48 * k + 16 * which + 16, cols] = value
                        if t in (1, 2, 3):
                            tails[which, t, k] = value
        for k in range(9):
            at = slice(48 * k + 32, 48 * k + 48)
            low = sub < 8
            xs[0, at, cols] = jnp.where(low, tails[0, 1, k], tails[1, 3, k])
            xs[1, at, cols] = jnp.where(low, tails[0, 2, k], tails[1, 2, k])
            xs[2, at, cols] = jnp.where(low, tails[1, 2, k], tails[0, 2, k])
            xs[3, at, cols] = jnp.where(low, tails[1, 1, k], tails[0, 3, k])

    def silu_of_double(h):
        return h + h * jnp.tanh(h)

    def store_rows(value, half, place, order):
        for p, q in enumerate(order):
            flat_out[pl.ds(64 * half + 16 * q + place, CH, stride=128), :] = value[CH * p : CH * (p + 1)]

    flat_out = out.reshape(CH * 128, 128)

    def t_copy(t):
        return remote(t_send.at[t], t_arrived.at[t], t_ssem.at[t], t_rsem.at[t], partner)

    def borders():
        to_south.wait()
        to_north.wait()
        for index in (1, 2, 3, 130, 131, 132):
            s1[index] = advance_row(s0, index)
        lax.fori_loop(7, 9, send_packs, 0)

        side_south.wait()
        side_north.wait()
        first, second = edge_values((0, 1))
        strips[0] = first
        strips[1] = jnp.where(lane < 16, second, strips[1])
        second, last = edge_values((8, 9))
        strips[8] = jnp.where(lane >= 112, second, strips[8])
        strips[9] = last
        keep_edges(2)
        keep_edges(3)
        z_copy(1).start()

    def network(t, xs, beside):
        halves, first = [], []
        for q in range(STRIPS):
            halves.append(jnp.dot(w1[q], xs[q], preferred_element_type=F32))
            if q == 1:
                beside[0]()
        for q in range(STRIPS):
            first.append(silu_of_double(halves[q]).astype(BF16))
            halves[q] = jnp.dot(w2[...], first[q], preferred_element_type=F32)
            if q == 1:
                beside[1]()
        beside[2]()
        for q in range(STRIPS):
            ys[256 * q : 256 * (q + 1), :] = silu_of_double(halves[q]).astype(BF16)
        tendency = jnp.dot(w3[...], ys[...], preferred_element_type=F32).astype(BF16)
        for u in range(2):
            t_send[t, u] = tendency[PACK:, 128 * u : 128 * (u + 1)]
        t_copy(t).start()
        for u in range(2):
            place = 15 * (1 - own) + d_own * (2 * t + u)
            value = moved_own[2 * t + 1 + u] + tendency[:PACK, 128 * u : 128 * (u + 1)].astype(F32)
            store_rows(value, own, place, (0, 1, 2, 3))

    z_copy(0).wait_recv()
    pack_copy(0).wait_recv()
    pack_copy(1).wait_recv()
    for slot in range(4):
        ingest(slot)
    for u in range(2):
        pick_neighbours(1 + u, u, xs_even)

    nothing = (lambda: None,) * 3

    def beside(t, xs):
        def prepare():
            keep_packs(t + 2, 0)
            ingest(2 * t + 4)
            ingest(2 * t + 5)

        return (
            prepare,
            lambda: pick_neighbours(2 * t + 3, 0, xs),
            lambda: pick_neighbours(2 * t + 4, 1, xs),
        )

    def physics(p, carry):
        for odd, (here, there) in enumerate(((xs_even, xs_odd), (xs_odd, xs_even))):
            t = 2 * p + odd
            pack_copy(t + 2).wait_recv()
            if odd:

                @pl.when(p == 0)
                def _():
                    borders()

                @pl.when(p == 2)
                def _():
                    z_copy(1).wait_recv()

            network(t, here, beside(t, there))
        return carry

    lax.fori_loop(0, STEPS // 2 - 1, physics, 0)
    pack_copy(STEPS).wait_recv()
    network(STEPS - 2, xs_even, beside(STEPS - 2, xs_odd))
    network(STEPS - 1, xs_odd, nothing)

    def finish(t, carry):
        t_copy(t).wait_recv()
        for u in range(2):
            place = 15 * (1 - sent) + d_sent * (2 * t + u)
            value = fix_edges(moved_sent[2 * t + 1 + u], z_sent[2], place) + t_arrived[t, u].astype(F32)
            store_rows(value, sent, place, (3, 2, 1, 0))
        return carry

    lax.fori_loop(0, STEPS, finish, 0)
    z_copy(0).wait_send()
    z_copy(1).wait_send()
    for s in range(SENDS):
        pack_copy(s).wait_send()
    for t in range(STEPS):
        t_copy(t).wait_send()


def shards(state, courant_x, courant_y, diffusion, neighbours, w_in, w_mid, w_out):
    levels, fields, single, cells_x, cells_y = state.shape
    chans = levels * fields
    anywhere = pl.BlockSpec(memory_space=pltpu.HBM)
    scalars = pl.BlockSpec(memory_space=pltpu.SMEM)
    vmem = pltpu.VMEM
    dma = pltpu.SemaphoreType.DMA
    updated = pl.pallas_call(
        kernel,
        out_shape=pltpu.VMEM((chans, cells_x, cells_y), F32),
        in_specs=[anywhere, scalars, scalars, scalars, anywhere, anywhere, anywhere, anywhere, anywhere],
        out_specs=pl.BlockSpec(memory_space=vmem),
        scratch_shapes=[
            vmem((CH, 128, 128), F32),
            vmem((134, CH, 128), F32),
            vmem((134, CH, 128), F32),
            vmem((5, CH, 128), F32),
            vmem((8, CH, 128), F32),
            vmem((2, 4, CH, 128), F32),
            vmem((4, CH, 128), F32),
            vmem((4, CH, 128), F32),
            vmem((10, 2, CH, 128), F32),
            vmem((10, CH, 128), F32),
            vmem((SLOTS, PACK, 128), F32),
            vmem((SLOTS, PACK, 128), F32),
            vmem((SLOTS, PACK, 128), BF16),
            vmem((SLOTS, PACK, 128), BF16),
            vmem((4, PACK, 128), F32),
            vmem((4, PACK, 128), F32),
            vmem((4, PACK, 128), BF16),
            vmem((4, PACK, 128), BF16),
            vmem((2, SLOTS, 3, PACK, 128), BF16),
            vmem((2, 16, 3, PACK, 128), BF16),
            vmem((STRIPS, KIN, 256), BF16),
            vmem((STRIPS, KIN, 256), BF16),
            vmem((STRIPS * 256, 256), BF16),
            vmem((360, 256), BF16),
            vmem((256, 256), BF16),
            vmem((40, 256), BF16),
            vmem((STRIPS, 256, KIN), BF16),
            vmem((256, 256), BF16),
            vmem((2 * PACK, STRIPS * 256), BF16),
            vmem((2, 64, 128), jnp.int32),
            vmem((STRIPS, 1, KIN), jnp.int32),
            vmem((STEPS, 2, PACK, 128), BF16),
            vmem((STEPS, 2, PACK, 128), BF16),
            dma((8,)),
            dma((6,)),
            dma((SENDS,)),
            dma((SENDS,)),
            dma((2,)),
            dma((2,)),
            dma((STEPS,)),
            dma((STEPS,)),
            dma((6,)),
            dma((6,)),
        ],
        compiler_params=pltpu.CompilerParams(
            collective_id=0, has_side_effects=True, vmem_limit_bytes=60900 * 1024
        ),
    )(
        state.reshape(chans, cells_x, cells_y),
        courant_x,
        courant_y,
        diffusion,
        neighbours.reshape(9, cells_x, cells_y),
        w_in,
        w_mid,
        w_out.T,
        jnp.asarray(feature_rows()),
    )
    return updated.reshape(levels, fields, single, cells_x, cells_y)


def solution(mesh):
    return jax.shard_map(
        shards,
        mesh=mesh,
        in_specs=(
            P("group", None, "tile", None, None),
            P("group"),
            P("group"),
            P(),
            P(None, "tile", None, None),
            P(),
            P(),
            P(),
        ),
        out_specs=P("group", None, "tile", None, None),
        check_vma=False,
    )
```
